128 devices in a mesh: row: 16 (over x, z_hi, core), col: 8 (over y, z_lo).
Axes of the slice: x: 4, y: 4, z: 4 (z_hi: 2, z_lo: 2; z = z_hi * 2 + z_lo), core: 2. Of those that a mesh axis runs over, the one named last changes fastest.
Arguments:
- waveform: bfloat16 [128, 1024, 8192], P(('row', 'col')), may hold values from -50 to 50, as said below
- valid_mask: int32 [128, 1024], P(('row', 'col')), may hold values 0 or 1
- band_starts: int32 [10], replicated, may hold values from 0 to 4080
- station_map: int32 [1024], replicated, may hold values from 0 to 1023, each once
Outputs:
- stacked: bfloat16 [2, 160, 1024, 1024], P(None, None, 'row', 'col')
The draws below stay inside these ranges and needn't reach their ends.
Inputs may be any that keep to these rules, and one draw needn't show every extreme that they name: `waveform`: entries are real samples whose per-trace scale varies from trace to trace. `band_starts`: each band's 16 bins lie below 4096. `station_map`: a permutation of the stations.
All inputs are finite; a program needn't handle non-finite values. No bound on the sum of `valid_mask` on one device may be relied on, other than what follows from the above.
Results may differ from the reference program's by a relative error of at most 0.0068.
Values may be sent and summed in bfloat16 or wider, within the bound.
No kernel may reach another device: no remote copies, remote signals or barrier semaphores. Data moves between devices by JAX's collectives and lax.ppermute only.
A program may use at most 128 MiB of HBM per device.

```python
import math
import jax
import jax.numpy as jnp
from jax import lax

L = 8192
BINS = 16
NBAND = 10
STATIONS = 1024
F = 160
WINDOWS = 128


def draw_waveform(key, part):
    key = jax.random.fold_in(key, 5)
    base_key, scale_key = jax.random.split(key)
    shape = (WINDOWS, STATIONS, L)
    base = jnp.clip(jax.random.normal(base_key, shape, jnp.float32), -5.0, 5.0)
    scales = jnp.exp(jax.random.uniform(scale_key, (WINDOWS, STATIONS, 1), jnp.float32, 0.0, math.log(10.0)))
    return (base * scales).astype(jnp.bfloat16)


def touch_ends(entries, own_key, smallest, largest):
    spot = [jax.random.randint(jax.random.fold_in(own_key, axis), (), 0, length) for axis, length in enumerate(entries.shape)]
    widest = entries.shape.index(max(entries.shape))
    beside = spot[:widest] + [(spot[widest] + 1) % entries.shape[widest]] + spot[widest + 1:]
    return entries.at[tuple(spot)].set(smallest).at[tuple(beside)].set(largest)


def setup_inputs(seed: int = 0) -> dict:
    key_of = jax.random.split(jax.random.key(seed), 5)
    waveform = draw_waveform(jax.random.fold_in(key_of[4], 71), 0)
    valid_mask = touch_ends((jax.random.randint(key_of[1], (WINDOWS, STATIONS), 0, 4) < 3).astype(jnp.int32), jax.random.fold_in(key_of[1], 1), 0, 1)
    band_starts = touch_ends(jax.random.randint(key_of[2], (NBAND,), 0, L // 2 - BINS + 1), jax.random.fold_in(key_of[2], 1), 0, (L // 2 - BINS + 1) - 1).astype(jnp.int32)
    station_map = jax.random.permutation(key_of[3], STATIONS).astype(jnp.int32)
    return dict(waveform=waveform, valid_mask=valid_mask, band_starts=band_starts, station_map=station_map)


def make_table(band_starts, length, bin_count):
    frequency = (band_starts[:, None] + jnp.arange(bin_count, dtype=jnp.int32)[None, :]).reshape(-1).astype(jnp.int32)
    samples = jnp.arange(length, dtype=jnp.int32)
    phase_index = frequency[:, None] * samples[None, :] % length
    angles = phase_index.astype(jnp.float32) * jnp.float32(2.0 * math.pi / length)
    scaling = jnp.float32(length ** (-0.5))
    return (jnp.concatenate([jnp.cos(angles), -jnp.sin(angles)], axis=0) * scaling).astype(jnp.bfloat16)

def whiten(spectra, mask_rows, band_count):
    count, double_bins, stations = spectra.shape
    half = double_bins // 2
    real_part = spectra[:, :half]
    imag_part = spectra[:, half:]
    power_bins = real_part * real_part + imag_part * imag_part
    band_mean = power_bins.reshape(count, band_count, half // band_count, stations).mean(axis=2, keepdims=True)
    band_mean = jnp.broadcast_to(band_mean, (count, band_count, half // band_count, stations)).reshape(count, half, stations)
    factor = mask_rows[:, None, :].astype(jnp.float32) / jnp.sqrt(power_bins + band_mean + 0.1)
    return jnp.concatenate([real_part * factor, imag_part * factor], axis=1).astype(jnp.bfloat16)

def reference(waveform, valid_mask, band_starts, station_map):
    dft_table = make_table(band_starts, L, BINS)

    def per_window(inputs):
        wave_rows, mask_row = inputs
        spectra = jnp.dot(dft_table, wave_rows.T, preferred_element_type=jnp.float32)
        sum_squares = lax.optimization_barrier(jnp.sum(jnp.square(wave_rows.astype(jnp.float32)), axis=1))
        rms_value = jnp.sqrt(sum_squares / L + 1e-06)
        spectra = spectra / rms_value[None, :]
        return whiten(spectra[None], mask_row[None], NBAND)[0]
    whitened = lax.map(per_window, (waveform, valid_mask))
    grid_order = whitened[:, :, station_map]
    scaling = jnp.float32(float(WINDOWS) ** (-0.5))

    def one_bin(index):
        real_part = lax.dynamic_index_in_dim(grid_order, index, 1, keepdims=False)
        imag_part = lax.dynamic_index_in_dim(grid_order, index + F, 1, keepdims=False)
        real_out = jnp.dot(real_part.T, real_part, preferred_element_type=jnp.float32) + jnp.dot(imag_part.T, imag_part, preferred_element_type=jnp.float32)
        imag_out = jnp.dot(real_part.T, imag_part, preferred_element_type=jnp.float32) - jnp.dot(imag_part.T, real_part, preferred_element_type=jnp.float32)
        return (jnp.stack([real_out, imag_out], axis=0) * scaling).astype(jnp.bfloat16)
    per_bin = lax.map(one_bin, jnp.arange(F, dtype=jnp.int32))
    return jnp.transpose(per_bin, (1, 0, 2, 3))
```

```python
import functools
import itertools
import math

import jax
import jax.numpy as jnp
from jax import lax
from jax.experimental import pallas as pl
from jax.experimental.pallas import tpu as pltpu
from jax.sharding import PartitionSpec as P

BINS = 16
AXES = ("row", "col")
SIZES = (4, 2, 2, 4, 2)
GROUPS = 8
CHUNKS = (8, 12)
VMEM = 56 * 1024 * 1024


def coordinates():
    row = lax.axis_index("row")
    col = lax.axis_index("col")
    x, z_hi, core = row // 4, row // 2 % 2, row % 2
    y, z_lo = col // 2, col % 2
    return x, y, z_hi * 2 + z_lo, core


def permute(array, move):
    pairs = []
    for source, (x, z_hi, core, y, z_lo) in enumerate(
        itertools.product(*(range(size) for size in SIZES))
    ):
        x2, y2, z2, core2 = move(x, y, z_hi * 2 + z_lo, core)
        target = (((x2 % 4 * 2 + z2 % 4 // 2) * 2 + core2 % 2) * 4 + y2 % 4) * 2 + z2 % 2
        pairs.append((source, target))
    return lax.ppermute(array, AXES, pairs)


def split_dot(left, right, dims):
    total = None
    for _ in range(3):
        term = right.astype(jnp.bfloat16)
        right = right - term.astype(jnp.float32)
        part = lax.dot_general(left, term, dims, preferred_element_type=jnp.float32)
        total = part if total is None else total + part
    return total


def spectra_kernel(
    place_ref, band_ref, wave_ref, mask_ref, map_ref, *refs, length, band_count, chunks
):
    outs = refs[: len(chunks) * GROUPS]
    table_ref, white_ref = refs[len(chunks) * GROUPS :]
    step = pl.program_id(0)
    bins = band_count * BINS
    width = wave_ref.shape[0]
    stations = white_ref.shape[1]
    lanes = 128

    @pl.when(step == 0)
    def _():
        band = lax.broadcasted_iota(jnp.int32, (bins, lanes), 0) // BINS
        lane = lax.broadcasted_iota(jnp.int32, (bins, lanes), 1)
        frequency = lax.broadcasted_iota(jnp.int32, (bins, lanes), 0) % BINS
        for b in range(band_count):
            frequency = frequency + jnp.where(band == b, band_ref[b], 0)
        unit = jnp.float32(2.0 * math.pi / length)
        scaling = jnp.float32(length ** (-0.5))
        fine = (frequency * lane % length).astype(jnp.float32) * unit
        coarse = (frequency * (lane * lanes % length) % length).astype(jnp.float32) * unit
        fine_cos = jnp.cos(fine) * scaling
        fine_sin = jnp.sin(fine) * scaling
        coarse_cos = jnp.cos(coarse)
        coarse_sin = jnp.sin(coarse)
        for part in range(length // lanes):
            c = coarse_cos[:, part : part + 1]
            s = coarse_sin[:, part : part + 1]
            columns = slice(part * lanes, (part + 1) * lanes)
            table_ref[:bins, columns] = (c * fine_cos - s * fine_sin).astype(jnp.bfloat16)
            table_ref[bins:, columns] = (-s * fine_cos - c * fine_sin).astype(jnp.bfloat16)

    spectra = lax.dot_general(
        table_ref[...], wave_ref[...], (((1,), (1,)), ((), ())), preferred_element_type=jnp.float32
    )
    squares = jnp.zeros((width, lanes), jnp.float32)
    for part in range(length // lanes):
        piece = wave_ref[:, part * lanes : (part + 1) * lanes].astype(jnp.float32)
        squares = squares + piece * piece
    ones = jnp.ones((8, lanes), jnp.bfloat16)
    total = split_dot(ones, squares, (((1,), (1,)), ((), ())))[:1]
    inverse = lax.rsqrt(total / length + 1e-06)
    real_part = spectra[:bins] * inverse
    imag_part = spectra[bins:] * inverse
    power = real_part * real_part + imag_part * imag_part
    banded = power.reshape(band_count, BINS, width)
    mean = jnp.broadcast_to(jnp.mean(banded, axis=1, keepdims=True), banded.shape)
    mask = mask_ref[...].astype(jnp.float32)
    factor = mask * lax.rsqrt(power + mean.reshape(bins, width) + 0.1)
    columns = pl.ds(pl.multiple_of(step * width, width), width)
    white_ref[:bins, columns] = (real_part * factor).astype(jnp.bfloat16)
    white_ref[bins:, columns] = (imag_part * factor).astype(jnp.bfloat16)

    @pl.when(step == pl.num_programs(0) - 1)
    def _():
        z, core = place_ref[2], place_ref[3]
        rows = 2 * bins
        goal = lax.broadcasted_iota(jnp.int32, (rows, 1), 0)
        source = jnp.zeros((rows, 1), jnp.int32)
        start = 0
        for nb in chunks:
            base = 2 * GROUPS * start
            local = goal - base
            slot = local // (2 * nb)
            within = local % (2 * nb)
            group = (z + slot // 2) % 4 * 2 + (core + slot) % 2
            picked = within // nb * bins + GROUPS * start + group * nb + within % nb
            inside = (local >= 0) & (local < 2 * GROUPS * nb)
            source = jnp.where(inside, picked, source)
            start += nb
        order = lax.broadcasted_iota(jnp.int32, (rows, rows), 1) == source
        order = order.astype(jnp.float32).astype(jnp.bfloat16)
        sorted_rows = jnp.dot(
            order, white_ref[...], preferred_element_type=jnp.float32
        ).astype(jnp.bfloat16)
        block = 256
        for first in range(0, stations, block):
            station = lax.broadcasted_iota(jnp.int32, (stations, block), 0)
            take = station == map_ref[:, first : first + block]
            take = take.astype(jnp.float32).astype(jnp.bfloat16)
            moved = jnp.dot(sorted_rows, take, preferred_element_type=jnp.float32)
            moved = moved.astype(jnp.bfloat16)
            row = 0
            for c, nb in enumerate(chunks):
                for slot in range(GROUPS):
                    outs[c * GROUPS + slot][:, first : first + block] = moved[row : row + 2 * nb]
                    row += 2 * nb


def make_spectra(place, waveform, valid_mask, band_starts, station_map, chunks):
    stations, length = waveform.shape
    band_count = band_starts.shape[0]
    rows = 2 * BINS * band_count
    width = 256
    shapes = [
        jax.ShapeDtypeStruct((2 * nb, stations), jnp.bfloat16) for nb in chunks for _ in range(GROUPS)
    ]
    smem = pl.BlockSpec(memory_space=pltpu.SMEM)
    return pl.pallas_call(
        functools.partial(spectra_kernel, length=length, band_count=band_count, chunks=chunks),
        grid=(stations // width,),
        in_specs=[
            smem,
            smem,
            pl.BlockSpec((width, length), lambda i: (i, 0)),
            pl.BlockSpec((1, width), lambda i: (0, i)),
            pl.BlockSpec((1, stations), lambda i: (0, 0)),
        ],
        out_specs=[pl.BlockSpec(s.shape, lambda i: (0, 0)) for s in shapes],
        out_shape=shapes,
        scratch_shapes=[
            pltpu.VMEM((rows, length), jnp.bfloat16),
            pltpu.VMEM((rows, stations), jnp.bfloat16),
        ],
        compiler_params=pltpu.CompilerParams(vmem_limit_bytes=VMEM),
        cost_estimate=pl.CostEstimate(
            flops=2 * rows * length * stations, bytes_accessed=2 * stations * length, transcendentals=0
        ),
        name="spectra",
    )(place, band_starts, waveform, valid_mask, station_map)


def weave_kernel(place_ref, *refs, nb):
    ins, outs, woven_ref = refs[:GROUPS], refs[GROUPS:-1], refs[-1]
    x, y = place_ref[0], place_ref[1]
    stacked = jnp.stack([ref[...].astype(jnp.float32) for ref in ins], axis=0)
    stacked = jnp.swapaxes(stacked, 0, 1)
    woven_ref[...] = jnp.concatenate([stacked[:nb], stacked[nb:]], axis=1).astype(jnp.bfloat16)
    block = outs[0].shape[2]
    for side, own in enumerate((x, y)):
        for k in range(4):
            first = pl.multiple_of((own + k) % 4 * block, block)
            outs[side * 4 + k][...] = woven_ref[:, :, pl.ds(first, block)]


def weave(place, slots, nb):
    stations = slots[0].shape[1]
    shape = jax.ShapeDtypeStruct((nb, 16, stations // 4), jnp.bfloat16)
    return pl.pallas_call(
        functools.partial(weave_kernel, nb=nb),
        in_specs=[pl.BlockSpec(memory_space=pltpu.SMEM)]
        + [pl.BlockSpec(memory_space=pltpu.VMEM)] * GROUPS,
        out_specs=[pl.BlockSpec(memory_space=pltpu.VMEM)] * 8,
        out_shape=[shape] * 8,
        scratch_shapes=[pltpu.VMEM((nb, 16, stations), jnp.bfloat16)],
        compiler_params=pltpu.CompilerParams(vmem_limit_bytes=VMEM),
        name="weave",
    )(place, *slots)


def product_kernel(place_ref, *refs, scaling):
    rows, cols, outs, scratch = refs[:4], refs[4:8], refs[8:16], refs[16]
    z, core = place_ref[2], place_ref[3]
    count = rows[0].shape[1]
    for j in range(count):
        left = jnp.concatenate([rows[ky][kx, j] for kx in range(4) for ky in range(4)], axis=0)
        pieces = [cols[kx][ky, j] for kx in range(4) for ky in range(4)]
        right = jnp.concatenate(pieces, axis=0)
        wide = right.astype(jnp.float32).reshape(16, 2, 8, right.shape[1])
        turned = jnp.concatenate([wide[:, 1:], -wide[:, :1]], axis=1)
        turned = turned.reshape(right.shape).astype(jnp.bfloat16)
        dims = (((0,), (0,)), ((), ()))
        for part, operand in enumerate((right, turned)):
            result = lax.dot_general(left, operand, dims, preferred_element_type=jnp.float32)
            scratch[part, j] = (result * scaling).astype(jnp.bfloat16)
    for slot in range(GROUPS):
        goal_z = (z + slot // 2) % 4
        first_row = pl.multiple_of(goal_z // 2 * 128 + (core + slot) % 2 * 64, 64)
        first_col = pl.multiple_of(goal_z % 2 * 128, 128)
        outs[slot][...] = scratch[:, :, pl.ds(first_row, 64), pl.ds(first_col, 128)]


def product(place, rows, cols, nb, scaling):
    per_step = 4
    block = rows[0].shape[-1]
    shape = jax.ShapeDtypeStruct((2, nb, 64, 128), jnp.bfloat16)
    spec = pl.BlockSpec((4, per_step, 16, block), lambda i: (0, i, 0, 0))
    return pl.pallas_call(
        functools.partial(product_kernel, scaling=scaling),
        grid=(nb // per_step,),
        in_specs=[pl.BlockSpec(memory_space=pltpu.SMEM)] + [spec] * 8,
        out_specs=[pl.BlockSpec((2, per_step, 64, 128), lambda i: (0, i, 0, 0))] * GROUPS,
        out_shape=[shape] * GROUPS,
        scratch_shapes=[pltpu.VMEM((2, per_step, block, block), jnp.bfloat16)],
        compiler_params=pltpu.CompilerParams(vmem_limit_bytes=VMEM),
        cost_estimate=pl.CostEstimate(
            flops=4 * nb * block**3, bytes_accessed=8 * nb * block * block * 2, transcendentals=0
        ),
        name="product",
    )(place, *rows, *cols)


def place_kernel(place_ref, *refs, start, nb, aliased):
    ins = refs[:GROUPS]
    out, sems = refs[GROUPS + aliased], refs[-1]
    z, core = place_ref[2], place_ref[3]
    copies = []
    for slot in range(GROUPS):
        group = (z + 4 - slot // 2) % 4 * 2 + (core + slot) % 2
        first = group * sum(CHUNKS) + start
        copies.append(pltpu.make_async_copy(ins[slot], out.at[:, pl.ds(first, nb)], sems.at[slot]))
    for copy in copies:
        copy.start()
    for copy in copies:
        copy.wait()


def place_blocks(place, slots, total, start, nb, shape):
    aliased = total is not None
    anywhere = pl.BlockSpec(memory_space=pl.ANY)
    operands = [place, *slots] + ([total] if aliased else [])
    return pl.pallas_call(
        functools.partial(place_kernel, start=start, nb=nb, aliased=aliased),
        in_specs=[pl.BlockSpec(memory_space=pltpu.SMEM)]
        + [pl.BlockSpec(memory_space=pltpu.VMEM)] * GROUPS
        + [anywhere] * aliased,
        out_specs=anywhere,
        out_shape=shape,
        scratch_shapes=[pltpu.SemaphoreType.DMA((GROUPS,))],
        input_output_aliases={len(operands) - 1: 0} if aliased else {},
        compiler_params=pltpu.CompilerParams(vmem_limit_bytes=VMEM),
        name="place",
    )(*operands)


def exchange(slots):
    return [slots[0]] + [
        permute(
            slots[slot],
            lambda x, y, z, core, slot=slot: (x, y, z + slot // 2, core + slot),
        )
        for slot in range(1, GROUPS)
    ]


def along(array, axis, k):
    if axis == "x":
        return permute(array, lambda x, y, z, core: (x + k, y, z, core))
    return permute(array, lambda x, y, z, core: (x, y + k, z, core))


def body(waveform, valid_mask, band_starts, station_map):
    place = jnp.stack(coordinates()).astype(jnp.int32)
    stations = waveform.shape[1]
    windows = waveform.shape[0] * lax.axis_size("row") * lax.axis_size("col")
    bins = BINS * band_starts.shape[0]
    scaling = float(windows) ** (-0.5)
    spectra = make_spectra(
        place, waveform[0], valid_mask, band_starts, station_map.reshape(1, stations), (bins // GROUPS,)
    )
    shape = jax.ShapeDtypeStruct((2, bins, 64, 128), jnp.bfloat16)
    woven = weave(place, exchange(spectra), bins // GROUPS)
    row_parts = [woven[0]] + [along(woven[k], "x", k) for k in (1, 2, 3)]
    col_parts = [woven[4]] + [along(woven[4 + k], "y", k) for k in (1, 2, 3)]
    total = None
    start = 0
    for nb in CHUNKS:
        row_shard = jnp.stack([part[start : start + nb] for part in row_parts], axis=0)
        col_shard = jnp.stack([part[start : start + nb] for part in col_parts], axis=0)
        rows = [row_shard] + [along(row_shard, "y", k) for k in (1, 2, 3)]
        cols = [col_shard] + [along(col_shard, "x", k) for k in (1, 2, 3)]
        blocks = exchange(product(place, rows, cols, nb, scaling))
        total = place_blocks(place, blocks, total, start, nb, shape)
        start += nb
    return total


def solution(mesh):
    placed = (P(AXES, None, None), P(AXES, None), P(), P())
    return jax.shard_map(
        body, mesh=mesh, in_specs=placed, out_specs=P(None, None, "row", "col"), check_vma=False
    )
```

```python
import functools
import itertools
import math

import jax
import jax.numpy as jnp
import numpy as np
from jax import lax
from jax.experimental import pallas as pl
from jax.experimental.pallas import tpu as pltpu
from jax.sharding import PartitionSpec as P

BINS = 16
AXES = ("row", "col")
SIZES = (4, 2, 2, 4, 2)
PARTS = (2, 3)
VMEM = 63 * 1024 * 1024


def device(x, y, z, core):
    return (((x % 4 * 2 + z % 4 // 2) * 2 + core % 2) * 4 + y % 4) * 2 + z % 2


def everywhere():
    return list(itertools.product(range(4), range(4), range(4), range(2)))


LINES = [
    [device(x, y, z, core) for x in range(4) for z in range(4) for core in range(2)]
    for y in range(4)
]


def exchange(array):
    return lax.all_to_all(array, AXES, 0, 0, axis_index_groups=LINES, tiled=True)


def gather(array):
    blocks = [array]
    for k in (1, 2, 3):
        pairs = [
            (device(x, y, z, core), device(x, y + k, z, core)) for x, y, z, core in everywhere()
        ]
        blocks.append(lax.ppermute(array, AXES, pairs))
    return blocks


def split_dot(left, right, dims):
    total = None
    for _ in range(3):
        term = right.astype(jnp.bfloat16)
        right = right - term.astype(jnp.float32)
        part = lax.dot_general(left, term, dims, preferred_element_type=jnp.float32)
        total = part if total is None else total + part
    return total


def turn(phase, length):
    quarter = length // 4
    phase = phase & (length - 1)
    quadrant = lax.shift_right_logical(phase + quarter // 2, quarter.bit_length() - 1)
    angle = (phase - quadrant * quarter).astype(jnp.float32) * jnp.float32(2.0 * math.pi / length)
    square = angle * angle
    sine = angle + angle * square * (
        -1.0 / 6 + square * (1.0 / 120 + square * (-1.0 / 5040 + square * (1.0 / 362880)))
    )
    cosine = 1.0 + square * (
        -0.5 + square * (1.0 / 24 + square * (-1.0 / 720 + square * (1.0 / 40320)))
    )
    odd = (quadrant & 1) == 1
    cos_value = jnp.where(odd, sine, cosine)
    sin_value = jnp.where(odd, cosine, sine)
    cos_value = jnp.where(((quadrant + 1) & 2) == 2, -cos_value, cos_value)
    sin_value = jnp.where((quadrant & 2) == 2, -sin_value, sin_value)
    return cos_value, sin_value


def spectra_kernel(
    band_ref, whole_ref, mask_ref, map_ref, order_ref, out_ref, *scratch, length, band_count
):
    table_ref, white_ref, waves_ref, sems = scratch
    step = pl.program_id(0)
    bins = band_count * BINS
    blocks, width, _ = waves_ref.shape
    copies = [
        pltpu.make_async_copy(
            whole_ref.at[pl.ds(i * width, width)], waves_ref.at[i], sems.at[i]
        )
        for i in range(blocks)
    ]
    stations = white_ref.shape[1]
    lanes = 128

    @pl.when(step == 0)
    def _():
        for copy in copies:
            copy.start()
        row = lax.broadcasted_iota(jnp.int32, (bins, lanes), 0)
        lane = lax.broadcasted_iota(jnp.int32, (bins, lanes), 1)
        frequency = row & (BINS - 1)
        for b in range(band_count):
            first = b * BINS
            inside = (row >= first) & (row < first + BINS)
            frequency = frequency + jnp.where(inside, band_ref[b], 0)
        fine_cos, fine_sin = turn(frequency * lane, length)
        coarse_cos, coarse_sin = turn(frequency * ((lane * lanes) & (length - 1)), length)
        scaling = jnp.float32(length ** (-0.5))
        fine_cos = fine_cos * scaling
        fine_sin = fine_sin * scaling
        for part in range(length // lanes):
            c = coarse_cos[:, part : part + 1]
            s = coarse_sin[:, part : part + 1]
            columns = slice(part * lanes, (part + 1) * lanes)
            table_ref[:bins, columns] = (c * fine_cos - s * fine_sin).astype(jnp.bfloat16)
            table_ref[bins:, columns] = (-s * fine_cos - c * fine_sin).astype(jnp.bfloat16)

    for i in range(blocks):
        pl.when(step == i)(copies[i].wait)
    wave_ref = waves_ref.at[step]
    spectra = lax.dot_general(
        table_ref[...], wave_ref[...], (((1,), (1,)), ((), ())), preferred_element_type=jnp.float32
    )
    squares = jnp.zeros((width, lanes), jnp.float32)
    for part in range(length // lanes):
        piece = wave_ref[:, part * lanes : (part + 1) * lanes].astype(jnp.float32)
        squares = squares + piece * piece
    ones = jnp.ones((8, lanes), jnp.bfloat16)
    total = split_dot(ones, squares, (((1,), (1,)), ((), ())))[:1]
    inverse = lax.rsqrt(total / length + 1e-06)
    real_part = spectra[:bins] * inverse
    imag_part = spectra[bins:] * inverse
    power = real_part * real_part + imag_part * imag_part
    banded = power.reshape(band_count, BINS, width)
    mean = jnp.broadcast_to(jnp.mean(banded, axis=1, keepdims=True), banded.shape)
    mask = mask_ref[...].astype(jnp.float32)
    factor = mask * lax.rsqrt(power + mean.reshape(bins, width) + 0.1)
    columns = pl.ds(pl.multiple_of(step * width, width), width)
    white_ref[:bins, columns] = (real_part * factor).astype(jnp.bfloat16)
    white_ref[bins:, columns] = (imag_part * factor).astype(jnp.bfloat16)

    @pl.when(step == pl.num_programs(0) - 1)
    def _():
        devices, share = out_ref.shape[0], out_ref.shape[1] * lanes // stations
        sorted_rows = jnp.dot(
            order_ref[...], white_ref[...], preferred_element_type=jnp.float32
        ).astype(jnp.bfloat16)
        block = 2 * lanes
        for first in range(0, stations, block):
            station = lax.broadcasted_iota(jnp.int32, (stations, block), 0)
            take = station == map_ref[:, first : first + block]
            take = take.astype(jnp.float32).astype(jnp.bfloat16)
            moved = jnp.dot(sorted_rows, take, preferred_element_type=jnp.float32)
            moved = moved.astype(jnp.bfloat16)
            for goal_device in range(devices):
                piece = moved[goal_device * share : (goal_device + 1) * share]
                for side in range(2):
                    row = (first // lanes + side) * share
                    out_ref[goal_device, row : row + share] = piece[
                        :, side * lanes : (side + 1) * lanes
                    ]


def make_spectra(waveform, valid_mask, band_starts, station_map, devices):
    stations, length = waveform.shape
    band_count = band_starts.shape[0]
    rows = 2 * BINS * band_count
    width = 256
    bins = rows // 2
    order = np.arange(rows).reshape(2, devices, bins // devices).transpose(1, 0, 2).reshape(-1)
    order = jnp.asarray(np.eye(rows, dtype=np.float32)[order], jnp.bfloat16)
    shape = (devices, rows // devices * stations // 128, 128)
    smem = pl.BlockSpec(memory_space=pltpu.SMEM)
    return pl.pallas_call(
        functools.partial(spectra_kernel, length=length, band_count=band_count),
        grid=(stations // width,),
        in_specs=[
            smem,
            pl.BlockSpec(memory_space=pl.ANY),
            pl.BlockSpec((1, width), lambda i: (0, i)),
            pl.BlockSpec((1, stations), lambda i: (0, 0)),
            pl.BlockSpec((rows, rows), lambda i: (0, 0)),
        ],
        out_specs=pl.BlockSpec(shape, lambda i: (0, 0, 0)),
        out_shape=jax.ShapeDtypeStruct(shape, jnp.bfloat16),
        scratch_shapes=[
            pltpu.VMEM((rows, length), jnp.bfloat16),
            pltpu.VMEM((rows, stations), jnp.bfloat16),
            pltpu.VMEM((stations // width, width, length), jnp.bfloat16),
            pltpu.SemaphoreType.DMA((stations // width,)),
        ],
        compiler_params=pltpu.CompilerParams(vmem_limit_bytes=VMEM),
        cost_estimate=pl.CostEstimate(
            flops=2 * rows * length * stations, bytes_accessed=2 * stations * length, transcendentals=0
        ),
        name="spectra",
    )(band_starts, waveform, valid_mask, station_map, order)


def weave_kernel(in_ref, *outs):
    lanes = in_ref.shape[2]
    stations = outs[0].shape[3]
    share = in_ref.shape[1] * lanes // stations
    woven = jnp.swapaxes(in_ref[...].astype(jnp.float32), 0, 1).astype(jnp.bfloat16)
    for block in range(stations // lanes):
        for part in range(2):
            row = block * share + part * share // 2
            for out in outs:
                for j in range(out.shape[1]):
                    out[part, j, :, block * lanes : (block + 1) * lanes] = woven[row]
                    row += 1


def weave(array, stations):
    whole = pl.BlockSpec(memory_space=pltpu.VMEM)
    windows = array.shape[0]
    shapes = [jax.ShapeDtypeStruct((2, nb, windows, stations), jnp.bfloat16) for nb in PARTS]
    return pl.pallas_call(
        weave_kernel,
        in_specs=[whole],
        out_specs=[whole] * len(shapes),
        out_shape=shapes,
        compiler_params=pltpu.CompilerParams(vmem_limit_bytes=VMEM),
        name="weave",
    )(array)


def product_kernel(y_ref, *refs, scaling):
    blocks, out = refs[:4], refs[4]
    width = 256
    columns = pl.ds(pl.multiple_of(y_ref[0] * width, width), width)
    pieces = [(block, part) for part in range(2) for block in blocks]
    left = jnp.concatenate([block[part, 0] for block, part in pieces], axis=0)
    right = [block[part, 0, :, columns] for block, part in pieces]
    turned = right[4:] + [-piece for piece in right[:4]]
    both = jnp.concatenate(
        [jnp.concatenate(right, axis=0), jnp.concatenate(turned, axis=0)], axis=1
    )
    dims = (((0,), (0,)), ((), ()))
    result = lax.dot_general(left, both, dims, preferred_element_type=jnp.float32)
    result = (result * scaling).astype(jnp.bfloat16)
    for group in range(out.shape[0]):
        first_row = group // 8 * 256 + group // 4 % 2 * 128 + group % 2 * 64
        for part in range(2):
            first_col = part * width + group // 2 % 2 * 128
            out[group, part, 0] = result[first_row : first_row + 64, first_col : first_col + 128]


def product(y, blocks, scaling, devices):
    _, nb, windows, stations = blocks[0].shape
    spec = pl.BlockSpec((2, 1, windows, stations), lambda i: (0, i, 0, 0))
    return pl.pallas_call(
        functools.partial(product_kernel, scaling=scaling),
        grid=(nb,),
        in_specs=[pl.BlockSpec(memory_space=pltpu.SMEM)] + [spec] * 4,
        out_specs=pl.BlockSpec((devices, 2, 1, 64, 128), lambda i: (0, 0, i, 0, 0)),
        out_shape=jax.ShapeDtypeStruct((devices, 2, nb, 64, 128), jnp.bfloat16),
        compiler_params=pltpu.CompilerParams(vmem_limit_bytes=VMEM),
        cost_estimate=pl.CostEstimate(
            flops=nb * 2**28, bytes_accessed=nb * 2**21, transcendentals=0
        ),
        name="product",
    )(y, *blocks)


def place_kernel(in_ref, *refs, start, stride):
    out, buffer, in_sems, out_sems = refs[-4:]
    devices, _, nb = buffer.shape[:3]
    arrivals = [
        pltpu.make_async_copy(in_ref.at[i], buffer.at[i], in_sems.at[i]) for i in range(devices)
    ]
    departures = [
        pltpu.make_async_copy(
            buffer.at[i], out.at[:, pl.ds(start + i * stride, nb)], out_sems.at[i]
        )
        for i in range(devices)
    ]
    for arrival in arrivals:
        arrival.start()
    for arrival, departure in zip(arrivals, departures):
        arrival.wait()
        departure.start()
    for departure in departures:
        departure.wait()


def place_blocks(array, total, start, stride, shape):
    anywhere = pl.BlockSpec(memory_space=pl.ANY)
    operands = [array] + ([] if total is None else [total])
    devices = array.shape[0]
    return pl.pallas_call(
        functools.partial(place_kernel, start=start, stride=stride),
        in_specs=[anywhere] * len(operands),
        out_specs=anywhere,
        out_shape=shape,
        scratch_shapes=[
            pltpu.VMEM(array.shape, array.dtype),
            pltpu.SemaphoreType.DMA((devices,)),
            pltpu.SemaphoreType.DMA((devices,)),
        ],
        input_output_aliases={} if total is None else {1: 0},
        compiler_params=pltpu.CompilerParams(vmem_limit_bytes=VMEM),
        name="place",
    )(*operands)


def body(waveform, valid_mask, band_starts, station_map):
    y = (lax.axis_index("col") // 2).astype(jnp.int32).reshape(1)
    stations = waveform.shape[1]
    windows = waveform.shape[0] * lax.axis_size("row") * lax.axis_size("col")
    bins = BINS * band_starts.shape[0]
    scaling = float(windows) ** (-0.5)
    devices = len(LINES[0])
    spectra = make_spectra(
        waveform[0], valid_mask, band_starts, station_map.reshape(1, stations), devices
    )
    woven = weave(exchange(spectra), stations)
    shape = jax.ShapeDtypeStruct((2, bins, 64, 128), jnp.bfloat16)
    total = None
    start = 0
    for part in woven:
        blocks = exchange(product(y, gather(part), scaling, devices))
        total = place_blocks(blocks, total, start, sum(PARTS), shape)
        start += part.shape[1]
    return total


def solution(mesh):
    placed = (P(AXES, None, None), P(AXES, None), P(), P())
    return jax.shard_map(
        body, mesh=mesh, in_specs=placed, out_specs=P(None, None, "row", "col"), check_vma=False
    )
```

```python
import functools
import itertools
import math

import jax
import jax.numpy as jnp
import numpy as np
from jax import lax
from jax.experimental import pallas as pl
from jax.experimental.pallas import tpu as pltpu
from jax.sharding import PartitionSpec as P

BINS = 16
AXES = ("row", "col")
SIZES = (4, 2, 2, 4, 2)
PARTS = (2, 3)
VMEM = 63 * 1024 * 1024


def device(x, y, z, core):
    return (((x % 4 * 2 + z % 4 // 2) * 2 + core % 2) * 4 + y % 4) * 2 + z % 2


PLANES = [
    [device(x, y, z, 0) for x in range(4) for z in range(4)] for y in range(4)
] + [
    [device(x, y, z, 1) for y in range(4) for z in range(4)] for x in range(4)
]


def own_place():
    row, col = lax.axis_index("row"), lax.axis_index("col")
    core = row % 2
    return core, core * (row // 4) + (1 - core) * (col // 2)


def exchange(array):
    return lax.all_to_all(array, AXES, 0, 0, axis_index_groups=PLANES, tiled=True)


def permute(array, move):
    pairs = [
        (device(*place), device(*move(*place)))
        for place in itertools.product(range(4), range(4), range(4), range(2))
    ]
    return lax.ppermute(array, AXES, pairs)


def swap(array):
    return permute(array, lambda x, y, z, core: (x, y, z, core + 1))


def gather(array):
    return [array] + [
        permute(array, lambda x, y, z, core: (x + k * core, y + k * (1 - core), z, core))
        for k in (1, 2, 3)
    ]


def split_dot(left, right, dims):
    total = None
    for _ in range(3):
        term = right.astype(jnp.bfloat16)
        right = right - term.astype(jnp.float32)
        part = lax.dot_general(left, term, dims, preferred_element_type=jnp.float32)
        total = part if total is None else total + part
    return total


def turn(phase, length):
    quarter = length // 4
    phase = phase & (length - 1)
    quadrant = lax.shift_right_logical(phase + quarter // 2, quarter.bit_length() - 1)
    angle = (phase - quadrant * quarter).astype(jnp.float32) * jnp.float32(2.0 * math.pi / length)
    square = angle * angle
    sine = angle + angle * square * (
        -1.0 / 6 + square * (1.0 / 120 + square * (-1.0 / 5040 + square * (1.0 / 362880)))
    )
    cosine = 1.0 + square * (
        -0.5 + square * (1.0 / 24 + square * (-1.0 / 720 + square * (1.0 / 40320)))
    )
    odd = (quadrant & 1) == 1
    cos_value = jnp.where(odd, sine, cosine)
    sin_value = jnp.where(odd, cosine, sine)
    cos_value = jnp.where(((quadrant + 1) & 2) == 2, -cos_value, cos_value)
    sin_value = jnp.where((quadrant & 2) == 2, -sin_value, sin_value)
    return cos_value, sin_value


def spectra_kernel(
    band_ref, whole_ref, mask_ref, map_ref, order_ref, *refs, length, band_count
):
    outs = refs[:2]
    table_ref, white_ref, waves_ref, sems = refs[2:]
    step = pl.program_id(0)
    bins = band_count * BINS
    blocks, width, _ = waves_ref.shape
    copies = [
        pltpu.make_async_copy(
            whole_ref.at[pl.ds(i * width, width)], waves_ref.at[i], sems.at[i]
        )
        for i in range(blocks)
    ]
    stations = white_ref.shape[1]
    lanes = 128

    @pl.when(step == 0)
    def _():
        for copy in copies:
            copy.start()
        row = lax.broadcasted_iota(jnp.int32, (bins, lanes), 0)
        lane = lax.broadcasted_iota(jnp.int32, (bins, lanes), 1)
        frequency = row & (BINS - 1)
        for b in range(band_count):
            first = b * BINS
            inside = (row >= first) & (row < first + BINS)
            frequency = frequency + jnp.where(inside, band_ref[b], 0)
        fine_cos, fine_sin = turn(frequency * lane, length)
        coarse_cos, coarse_sin = turn(frequency * ((lane * lanes) & (length - 1)), length)
        scaling = jnp.float32(length ** (-0.5))
        fine_cos = fine_cos * scaling
        fine_sin = fine_sin * scaling
        odd = (frequency & 1) == 1
        half = length // 2
        for part in range(half // lanes):
            c = coarse_cos[:, part : part + 1]
            s = coarse_sin[:, part : part + 1]
            real_part = c * fine_cos - s * fine_sin
            imag_part = -s * fine_cos - c * fine_sin
            first = part * lanes
            near, far = slice(first, first + lanes), slice(half + first, half + first + lanes)
            table_ref[:bins, near] = real_part.astype(jnp.bfloat16)
            table_ref[bins:, near] = imag_part.astype(jnp.bfloat16)
            table_ref[:bins, far] = jnp.where(odd, -real_part, real_part).astype(jnp.bfloat16)
            table_ref[bins:, far] = jnp.where(odd, -imag_part, imag_part).astype(jnp.bfloat16)

    for i in range(blocks):
        pl.when(step == i)(copies[i].wait)
    wave_ref = waves_ref.at[step]
    spectra = lax.dot_general(
        table_ref[...], wave_ref[...], (((1,), (1,)), ((), ())), preferred_element_type=jnp.float32
    )
    squares = jnp.zeros((width, lanes), jnp.float32)
    for part in range(length // lanes):
        piece = wave_ref[:, part * lanes : (part + 1) * lanes].astype(jnp.float32)
        squares = squares + piece * piece
    ones = jnp.ones((8, lanes), jnp.bfloat16)
    total = split_dot(ones, squares, (((1,), (1,)), ((), ())))[:1]
    inverse = lax.rsqrt(total / length + 1e-06)
    real_part = spectra[:bins] * inverse
    imag_part = spectra[bins:] * inverse
    power = real_part * real_part + imag_part * imag_part
    banded = power.reshape(band_count, BINS, width)
    mean = jnp.broadcast_to(jnp.mean(banded, axis=1, keepdims=True), banded.shape)
    mask = mask_ref[...].astype(jnp.float32)
    factor = mask * lax.rsqrt(power + mean.reshape(bins, width) + 0.1)
    columns = pl.ds(pl.multiple_of(step * width, width), width)
    white_ref[:bins, columns] = (real_part * factor).astype(jnp.bfloat16)
    white_ref[bins:, columns] = (imag_part * factor).astype(jnp.bfloat16)

    @pl.when(step == pl.num_programs(0) - 1)
    def _():
        sorted_rows = jnp.dot(
            order_ref[own_place()[0]], white_ref[...], preferred_element_type=jnp.float32
        ).astype(jnp.bfloat16)
        block = 2 * lanes
        for first in range(0, stations, block):
            station = lax.broadcasted_iota(jnp.int32, (stations, block), 0)
            take = station == map_ref[:, first : first + block]
            take = take.astype(jnp.float32).astype(jnp.bfloat16)
            moved = jnp.dot(sorted_rows, take, preferred_element_type=jnp.float32)
            moved = moved.astype(jnp.bfloat16)
            count = 0
            for out in outs:
                share = out.shape[1] * lanes // stations
                for goal in range(out.shape[0]):
                    piece = moved[count : count + share]
                    for side in range(2):
                        row = (first // lanes + side) * share
                        out[goal, row : row + share] = piece[:, side * lanes : (side + 1) * lanes]
                    count += share


def make_spectra(waveform, valid_mask, band_starts, station_map, devices):
    stations, length = waveform.shape
    band_count = band_starts.shape[0]
    rows = 2 * BINS * band_count
    width = 256
    halves = []
    for half in range(2):
        first = half * rows // 4
        pieces = []
        for nb in PARTS:
            pieces.append(np.arange(first, first + nb * devices).reshape(devices, 1, nb))
            first += nb * devices
        both = np.concatenate(pieces, axis=2) + np.array([[0], [rows // 2]])
        halves.append(both.reshape(-1))
    order = np.stack([np.concatenate(halves), np.concatenate(halves[::-1])])
    order = jnp.asarray(np.eye(rows, dtype=np.float32)[order], jnp.bfloat16)
    shape = (devices, rows // 2 // devices * stations // 128, 128)
    smem = pl.BlockSpec(memory_space=pltpu.SMEM)
    return pl.pallas_call(
        functools.partial(spectra_kernel, length=length, band_count=band_count),
        grid=(stations // width,),
        in_specs=[
            smem,
            pl.BlockSpec(memory_space=pl.ANY),
            pl.BlockSpec((1, width), lambda i: (0, i)),
            pl.BlockSpec((1, stations), lambda i: (0, 0)),
            pl.BlockSpec((2, rows, rows), lambda i: (0, 0, 0)),
        ],
        out_specs=[pl.BlockSpec(shape, lambda i: (0, 0, 0))] * 2,
        out_shape=[jax.ShapeDtypeStruct(shape, jnp.bfloat16)] * 2,
        scratch_shapes=[
            pltpu.VMEM((rows, length), jnp.bfloat16),
            pltpu.VMEM((rows, stations), jnp.bfloat16),
            pltpu.VMEM((stations // width, width, length), jnp.bfloat16),
            pltpu.SemaphoreType.DMA((stations // width,)),
        ],
        compiler_params=pltpu.CompilerParams(vmem_limit_bytes=VMEM),
        cost_estimate=pl.CostEstimate(
            flops=2 * rows * length * stations, bytes_accessed=2 * stations * length, transcendentals=0
        ),
        name="spectra",
    )(band_starts, waveform, valid_mask, station_map, order)


def weave_kernel(in_ref, *outs):
    lanes = in_ref.shape[2]
    stations = outs[0].shape[3]
    share = in_ref.shape[1] * lanes // stations
    woven = jnp.swapaxes(in_ref[...].astype(jnp.float32), 0, 1).astype(jnp.bfloat16)
    for block in range(stations // lanes):
        for part in range(2):
            row = block * share + part * share // 2
            for out in outs:
                for j in range(out.shape[1]):
                    out[part, j, :, block * lanes : (block + 1) * lanes] = woven[row]
                    row += 1


def weave(array, stations):
    whole = pl.BlockSpec(memory_space=pltpu.VMEM)
    windows = array.shape[0]
    shapes = [jax.ShapeDtypeStruct((2, nb, windows, stations), jnp.bfloat16) for nb in PARTS]
    return pl.pallas_call(
        weave_kernel,
        in_specs=[whole],
        out_specs=[whole] * len(shapes),
        out_shape=shapes,
        compiler_params=pltpu.CompilerParams(vmem_limit_bytes=VMEM),
        name="weave",
    )(array)


def product_kernel(*refs, scaling):
    blocks, out = refs[:4], refs[4]
    core, block = own_place()
    width = 256
    columns = pl.ds(pl.multiple_of(block * width, width), width)

    def multiply(left, right):
        turned = right[4:] + [-piece for piece in right[:4]]
        both = jnp.concatenate(
            [jnp.concatenate(right, axis=0), jnp.concatenate(turned, axis=0)], axis=1
        )
        dims = (((0,), (0,)), ((), ()))
        result = lax.dot_general(
            jnp.concatenate(left, axis=0), both, dims, preferred_element_type=jnp.float32
        )
        return (result * scaling).astype(jnp.bfloat16)

    def store(group, first_row, first_col, result):
        size = result.shape[1] // 2
        for part in range(2):
            for goal_core in range(2):
                row, col = first_row + goal_core * 64, part * size + first_col
                out[group, goal_core, part, 0] = result[row : row + 64, col : col + 128]

    whole = [block[part, 0] for part in range(2) for block in blocks]
    narrow = [block[part, 0, :, columns] for part in range(2) for block in blocks]

    @pl.when(core == 0)
    def _():
        result = multiply(whole, narrow)
        for group in range(16):
            x, z_hi, z_lo = group // 4, group // 2 % 2, group % 2
            store(group, x * 256 + z_hi * 128, z_lo * 128, result)

    @pl.when(core == 1)
    def _():
        result = multiply(narrow, whole)
        for group in range(16):
            y, z_hi, z_lo = group // 4, group // 2 % 2, group % 2
            store(group, z_hi * 128, y * 256 + z_lo * 128, result)


def product(blocks, scaling, devices):
    _, nb, windows, stations = blocks[0].shape
    spec = pl.BlockSpec((2, 1, windows, stations), lambda i: (0, i, 0, 0))
    return pl.pallas_call(
        functools.partial(product_kernel, scaling=scaling),
        grid=(nb,),
        in_specs=[spec] * 4,
        out_specs=pl.BlockSpec((devices, 2, 2, 1, 64, 128), lambda i: (0, 0, 0, i, 0, 0)),
        out_shape=jax.ShapeDtypeStruct((devices, 2, 2, nb, 64, 128), jnp.bfloat16),
        compiler_params=pltpu.CompilerParams(vmem_limit_bytes=VMEM),
        cost_estimate=pl.CostEstimate(
            flops=nb * 2**28, bytes_accessed=nb * 2**21, transcendentals=0
        ),
        name="product",
    )(*blocks)


def place_kernel(in_ref, *refs, start, half_bins, own):
    out, buffer, in_sems, out_sems = refs[-4:]
    devices, nb = in_ref.shape[0], in_ref.shape[3]
    core, _ = own_place()
    first = start + (core if own else 1 - core) * half_bins
    arrivals = [
        pltpu.make_async_copy(
            in_ref.at[i, core], buffer.at[:, pl.ds(i * nb, nb)], in_sems.at[i]
        )
        for i in range(devices)
    ]
    parts = out_sems.shape[0]
    size = devices // parts * nb
    departures = [
        pltpu.make_async_copy(
            buffer.at[:, pl.ds(i * size, size)],
            out.at[:, pl.ds(first + i * size, size)],
            out_sems.at[i],
        )
        for i in range(parts)
    ]
    for arrival in arrivals:
        arrival.start()
    for i in range(parts):
        for arrival in arrivals[i * devices // parts : (i + 1) * devices // parts]:
            arrival.wait()
        departures[i].start()
    for departure in departures:
        departure.wait()


def place_blocks(array, total, start, shape, own):
    anywhere = pl.BlockSpec(memory_space=pl.ANY)
    operands = [array] + ([] if total is None else [total])
    devices, _, parts, nb, rows, cols = array.shape
    return pl.pallas_call(
        functools.partial(place_kernel, start=start, half_bins=shape.shape[1] // 2, own=own),
        in_specs=[anywhere] * len(operands),
        out_specs=anywhere,
        out_shape=shape,
        scratch_shapes=[
            pltpu.VMEM((parts, devices * nb, rows, cols), array.dtype),
            pltpu.SemaphoreType.DMA((devices,)),
            pltpu.SemaphoreType.DMA((2,)),
        ],
        input_output_aliases={} if total is None else {1: 0},
        compiler_params=pltpu.CompilerParams(vmem_limit_bytes=VMEM),
        name="place",
    )(*operands)


def body(waveform, valid_mask, band_starts, station_map):
    stations = waveform.shape[1]
    windows = waveform.shape[0] * lax.axis_size("row") * lax.axis_size("col")
    bins = BINS * band_starts.shape[0]
    scaling = float(windows) ** (-0.5)
    devices = len(PLANES[0])
    own, other = make_spectra(
        waveform[0], valid_mask, band_starts, station_map.reshape(1, stations), devices
    )
    spectra = exchange(jnp.stack([own, swap(other)], axis=1))
    woven = weave(spectra.reshape(2 * devices, *own.shape[1:]), stations)
    shape = jax.ShapeDtypeStruct((2, bins, 64, 128), jnp.bfloat16)
    total = None
    start = 0
    for part in woven:
        blocks = exchange(product(gather(part), scaling, devices))
        if total is not None:
            total, blocks = lax.optimization_barrier((total, blocks))
        given = swap(blocks)
        total = place_blocks(blocks, total, start, shape, True)
        total = place_blocks(given, total, start, shape, False)
        start += part.shape[1] * devices
    return total


def solution(mesh):
    placed = (P(AXES, None, None), P(AXES, None), P(), P())
    return jax.shard_map(
        body, mesh=mesh, in_specs=placed, out_specs=P(None, None, "row", "col"), check_vma=False
    )
```

```python
import functools
import itertools
import math

import jax
import jax.numpy as jnp
import numpy as np
from jax import lax
from jax.experimental import pallas as pl
from jax.experimental.pallas import tpu as pltpu
from jax.sharding import PartitionSpec as P

BINS = 16
AXES = ("row", "col")
SIZES = (4, 2, 2, 4, 2)
PARTS = (2, 3)
VMEM = 63 * 1024 * 1024


def device(x, y, z, core):
    return (((x % 4 * 2 + z % 4 // 2) * 2 + core % 2) * 4 + y % 4) * 2 + z % 2


PLANES = [
    [device(x, y, z, 0) for x in range(4) for z in range(4)] for y in range(4)
] + [
    [device(x, y, z, 1) for y in range(4) for z in range(4)] for x in range(4)
]


def own_place():
    row, col = lax.axis_index("row"), lax.axis_index("col")
    core = row % 2
    return core, core * (row // 4) + (1 - core) * (col // 2)


def exchange(array):
    return lax.all_to_all(array, AXES, 0, 0, axis_index_groups=PLANES, tiled=True)


def permute(array, move):
    pairs = [
        (device(*place), device(*move(*place)))
        for place in itertools.product(range(4), range(4), range(4), range(2))
    ]
    return lax.ppermute(array, AXES, pairs)


def swap(array):
    return permute(array, lambda x, y, z, core: (x, y, z, core + 1))


def gather(array):
    return [array] + [
        permute(array, lambda x, y, z, core: (x + k * core, y + k * (1 - core), z, core))
        for k in (1, 2, 3)
    ]


def split_dot(left, right, dims):
    total = None
    for _ in range(3):
        term = right.astype(jnp.bfloat16)
        right = right - term.astype(jnp.float32)
        part = lax.dot_general(left, term, dims, preferred_element_type=jnp.float32)
        total = part if total is None else total + part
    return total


def turn(phase, length):
    quarter = length // 4
    phase = phase & (length - 1)
    quadrant = lax.shift_right_logical(phase + quarter // 2, quarter.bit_length() - 1)
    angle = (phase - quadrant * quarter).astype(jnp.float32) * jnp.float32(2.0 * math.pi / length)
    square = angle * angle
    sine = angle + angle * square * (
        -1.0 / 6 + square * (1.0 / 120 + square * (-1.0 / 5040 + square * (1.0 / 362880)))
    )
    cosine = 1.0 + square * (
        -0.5 + square * (1.0 / 24 + square * (-1.0 / 720 + square * (1.0 / 40320)))
    )
    odd = (quadrant & 1) == 1
    cos_value = jnp.where(odd, sine, cosine)
    sin_value = jnp.where(odd, cosine, sine)
    cos_value = jnp.where(((quadrant + 1) & 2) == 2, -cos_value, cos_value)
    sin_value = jnp.where((quadrant & 2) == 2, -sin_value, sin_value)
    return cos_value, sin_value


def spectra_kernel(
    band_ref, whole_ref, mask_ref, map_ref, order_ref, *refs, length, band_count
):
    outs = refs[:2]
    table_ref, white_ref, waves_ref, sems = refs[2:]
    step = pl.program_id(0)
    bins = band_count * BINS
    blocks, width, _ = waves_ref.shape
    copies = [
        pltpu.make_async_copy(
            whole_ref.at[pl.ds(i * width, width)], waves_ref.at[i], sems.at[i]
        )
        for i in range(blocks)
    ]
    stations = white_ref.shape[1]
    lanes = 128

    @pl.when(step == 0)
    def _():
        for copy in copies:
            copy.start()
        row = lax.broadcasted_iota(jnp.int32, (bins, lanes), 0)
        lane = lax.broadcasted_iota(jnp.int32, (bins, lanes), 1)
        frequency = row & (BINS - 1)
        for b in range(band_count):
            first = b * BINS
            inside = (row >= first) & (row < first + BINS)
            frequency = frequency + jnp.where(inside, band_ref[b], 0)
        fine_cos, fine_sin = turn(frequency * lane, length)
        coarse_cos, coarse_sin = turn(frequency * ((lane * lanes) & (length - 1)), length)
        scaling = jnp.float32(length ** (-0.5))
        fine_cos = fine_cos * scaling
        fine_sin = fine_sin * scaling
        odd = (frequency & 1) == 1
        half = length // 2
        for part in range(half // lanes):
            c = coarse_cos[:, part : part + 1]
            s = coarse_sin[:, part : part + 1]
            real_part = c * fine_cos - s * fine_sin
            imag_part = -s * fine_cos - c * fine_sin
            first = part * lanes
            near, far = slice(first, first + lanes), slice(half + first, half + first + lanes)
            table_ref[:bins, near] = real_part.astype(jnp.bfloat16)
            table_ref[bins:, near] = imag_part.astype(jnp.bfloat16)
            table_ref[:bins, far] = jnp.where(odd, -real_part, real_part).astype(jnp.bfloat16)
            table_ref[bins:, far] = jnp.where(odd, -imag_part, imag_part).astype(jnp.bfloat16)

    for i in range(blocks):
        pl.when(step == i)(copies[i].wait)
    wave_ref = waves_ref.at[step]
    spectra = lax.dot_general(
        table_ref[...], wave_ref[...], (((1,), (1,)), ((), ())), preferred_element_type=jnp.float32
    )
    squares = jnp.zeros((width, lanes), jnp.float32)
    for part in range(length // lanes):
        piece = wave_ref[:, part * lanes : (part + 1) * lanes].astype(jnp.float32)
        squares = squares + piece * piece
    ones = jnp.ones((8, lanes), jnp.bfloat16)
    total = split_dot(ones, squares, (((1,), (1,)), ((), ())))[:1]
    inverse = lax.rsqrt(total / length + 1e-06)
    real_part = spectra[:bins] * inverse
    imag_part = spectra[bins:] * inverse
    power = real_part * real_part + imag_part * imag_part
    banded = power.reshape(band_count, BINS, width)
    mean = jnp.broadcast_to(jnp.mean(banded, axis=1, keepdims=True), banded.shape)
    mask = mask_ref[...].astype(jnp.float32)
    factor = mask * lax.rsqrt(power + mean.reshape(bins, width) + 0.1)
    columns = pl.ds(pl.multiple_of(step * width, width), width)
    white_ref[:bins, columns] = (real_part * factor).astype(jnp.bfloat16)
    white_ref[bins:, columns] = (imag_part * factor).astype(jnp.bfloat16)

    @pl.when(step == pl.num_programs(0) - 1)
    def _():
        sorted_rows = jnp.dot(
            order_ref[own_place()[0]], white_ref[...], preferred_element_type=jnp.float32
        ).astype(jnp.bfloat16)
        block = 2 * lanes
        for first in range(0, stations, block):
            station = lax.broadcasted_iota(jnp.int32, (stations, block), 0)
            take = station == map_ref[:, first : first + block]
            take = take.astype(jnp.float32).astype(jnp.bfloat16)
            moved = jnp.dot(sorted_rows, take, preferred_element_type=jnp.float32)
            moved = moved.astype(jnp.bfloat16)
            count = 0
            for out in outs:
                share = out.shape[1] * lanes // stations
                for goal in range(out.shape[0]):
                    piece = moved[count : count + share]
                    for side in range(2):
                        row = (first // lanes + side) * share
                        out[goal, row : row + share] = piece[:, side * lanes : (side + 1) * lanes]
                    count += share


def make_spectra(waveform, valid_mask, band_starts, station_map, devices):
    stations, length = waveform.shape
    band_count = band_starts.shape[0]
    rows = 2 * BINS * band_count
    width = 256
    halves = []
    for half in range(2):
        first = half * rows // 4
        pieces = []
        for nb in PARTS:
            pieces.append(np.arange(first, first + nb * devices).reshape(devices, 1, nb))
            first += nb * devices
        both = np.concatenate(pieces, axis=2) + np.array([[0], [rows // 2]])
        halves.append(both.reshape(-1))
    order = np.stack([np.concatenate(halves), np.concatenate(halves[::-1])])
    order = jnp.asarray(np.eye(rows, dtype=np.float32)[order], jnp.bfloat16)
    shape = (devices, rows // 2 // devices * stations // 128, 128)
    smem = pl.BlockSpec(memory_space=pltpu.SMEM)
    return pl.pallas_call(
        functools.partial(spectra_kernel, length=length, band_count=band_count),
        grid=(stations // width,),
        in_specs=[
            smem,
            pl.BlockSpec(memory_space=pl.ANY),
            pl.BlockSpec((1, width), lambda i: (0, i)),
            pl.BlockSpec((1, stations), lambda i: (0, 0)),
            pl.BlockSpec((2, rows, rows), lambda i: (0, 0, 0)),
        ],
        out_specs=[pl.BlockSpec(shape, lambda i: (0, 0, 0))] * 2,
        out_shape=[jax.ShapeDtypeStruct(shape, jnp.bfloat16)] * 2,
        scratch_shapes=[
            pltpu.VMEM((rows, length), jnp.bfloat16),
            pltpu.VMEM((rows, stations), jnp.bfloat16),
            pltpu.VMEM((stations // width, width, length), jnp.bfloat16),
            pltpu.SemaphoreType.DMA((stations // width,)),
        ],
        compiler_params=pltpu.CompilerParams(vmem_limit_bytes=VMEM),
        cost_estimate=pl.CostEstimate(
            flops=2 * rows * length * stations, bytes_accessed=2 * stations * length, transcendentals=0
        ),
        name="spectra",
    )(band_starts, waveform, valid_mask, station_map, order)


def weave_kernel(in_ref, *outs):
    lanes = in_ref.shape[2]
    stations = outs[0].shape[3]
    share = in_ref.shape[1] * lanes // stations
    woven = jnp.swapaxes(in_ref[...].astype(jnp.float32), 0, 1).astype(jnp.bfloat16)
    for block in range(stations // lanes):
        for part in range(2):
            row = block * share + part * share // 2
            for out in outs:
                for j in range(out.shape[1]):
                    out[part, j, :, block * lanes : (block + 1) * lanes] = woven[row]
                    row += 1


def weave(array, stations):
    whole = pl.BlockSpec(memory_space=pltpu.VMEM)
    windows = array.shape[0]
    shapes = [jax.ShapeDtypeStruct((2, nb, windows, stations), jnp.bfloat16) for nb in PARTS]
    return pl.pallas_call(
        weave_kernel,
        in_specs=[whole],
        out_specs=[whole] * len(shapes),
        out_shape=shapes,
        compiler_params=pltpu.CompilerParams(vmem_limit_bytes=VMEM),
        name="weave",
    )(array)


def product_kernel(*refs, scaling):
    blocks, goal, out, sems = refs[:4], refs[4], refs[5], refs[6]
    copies = []
    core, block = own_place()
    width = 256
    columns = pl.ds(pl.multiple_of(block * width, width), width)

    def multiply(left, right):
        turned = right[4:] + [-piece for piece in right[:4]]
        both = jnp.concatenate(
            [jnp.concatenate(right, axis=0), jnp.concatenate(turned, axis=0)], axis=1
        )
        dims = (((0,), (0,)), ((), ()))
        result = lax.dot_general(
            jnp.concatenate(left, axis=0), both, dims, preferred_element_type=jnp.float32
        )
        return (result * scaling).astype(jnp.bfloat16)

    def store(group, j, first_row, first_col, result):
        size = result.shape[1] // 2
        for part in range(2):
            for goal_core in range(2):
                row, col = first_row + goal_core * 64, part * size + first_col
                out[group, goal_core, part, j] = result[row : row + 64, col : col + 128]

    for j in range(out.shape[3]):
        whole = [block[part, j] for part in range(2) for block in blocks]
        narrow = [block[part, j, :, columns] for part in range(2) for block in blocks]

        @pl.when(core == 0)
        def _(j=j, whole=whole, narrow=narrow):
            result = multiply(whole, narrow)
            for group in range(16):
                x, z_hi, z_lo = group // 4, group // 2 % 2, group % 2
                store(group, j, x * 256 + z_hi * 128, z_lo * 128, result)

        @pl.when(core == 1)
        def _(j=j, whole=whole, narrow=narrow):
            result = multiply(narrow, whole)
            for group in range(16):
                y, z_hi, z_lo = group // 4, group // 2 % 2, group % 2
                store(group, j, z_hi * 128, y * 256 + z_lo * 128, result)

        copies.append(
            pltpu.make_async_copy(out.at[:, :, :, j], goal.at[:, :, :, j], sems.at[j])
        )
        copies[j].start()
    for copy in copies:
        copy.wait()


def product(blocks, scaling, devices):
    _, nb, windows, stations = blocks[0].shape
    spec = pl.BlockSpec((2, nb, windows, stations), lambda i: (0, 0, 0, 0))
    return pl.pallas_call(
        functools.partial(product_kernel, scaling=scaling),
        grid=(1,),
        in_specs=[spec] * 4,
        out_specs=pl.BlockSpec(memory_space=pl.ANY),
        scratch_shapes=[
            pltpu.VMEM((devices, 2, 2, nb, 64, 128), jnp.bfloat16),
            pltpu.SemaphoreType.DMA((nb,)),
        ],
        out_shape=jax.ShapeDtypeStruct((devices, 2, 2, nb, 64, 128), jnp.bfloat16),
        compiler_params=pltpu.CompilerParams(vmem_limit_bytes=VMEM),
        cost_estimate=pl.CostEstimate(
            flops=nb * 2**28, bytes_accessed=nb * 2**21, transcendentals=0
        ),
        name="product",
    )(*blocks)


def place_kernel(in_ref, *refs, start, half_bins, own):
    out, buffer, in_sems, out_sems = refs[-4:]
    devices, nb = in_ref.shape[0], in_ref.shape[3]
    core, _ = own_place()
    first = start + (core if own else 1 - core) * half_bins
    arrivals = [
        pltpu.make_async_copy(
            in_ref.at[i, core], buffer.at[:, pl.ds(i * nb, nb)], in_sems.at[i]
        )
        for i in range(devices)
    ]
    parts = out_sems.shape[0]
    size = devices // parts * nb
    departures = [
        pltpu.make_async_copy(
            buffer.at[:, pl.ds(i * size, size)],
            out.at[:, pl.ds(first + i * size, size)],
            out_sems.at[i],
        )
        for i in range(parts)
    ]
    for arrival in arrivals:
        arrival.start()
    for i in range(parts):
        for arrival in arrivals[i * devices // parts : (i + 1) * devices // parts]:
            arrival.wait()
        departures[i].start()
    for departure in departures:
        departure.wait()


def place_blocks(array, total, start, shape, own):
    anywhere = pl.BlockSpec(memory_space=pl.ANY)
    operands = [array] + ([] if total is None else [total])
    devices, _, parts, nb, rows, cols = array.shape
    return pl.pallas_call(
        functools.partial(place_kernel, start=start, half_bins=shape.shape[1] // 2, own=own),
        in_specs=[anywhere] * len(operands),
        out_specs=anywhere,
        out_shape=shape,
        scratch_shapes=[
            pltpu.VMEM((parts, devices * nb, rows, cols), array.dtype),
            pltpu.SemaphoreType.DMA((devices,)),
            pltpu.SemaphoreType.DMA((4,)),
        ],
        input_output_aliases={} if total is None else {1: 0},
        compiler_params=pltpu.CompilerParams(vmem_limit_bytes=VMEM),
        name="place",
    )(*operands)


def body(waveform, valid_mask, band_starts, station_map):
    stations = waveform.shape[1]
    windows = waveform.shape[0] * lax.axis_size("row") * lax.axis_size("col")
    bins = BINS * band_starts.shape[0]
    scaling = float(windows) ** (-0.5)
    devices = len(PLANES[0])
    own, other = make_spectra(
        waveform[0], valid_mask, band_starts, station_map.reshape(1, stations), devices
    )
    spectra = exchange(jnp.stack([own, swap(other)], axis=1))
    woven = weave(spectra.reshape(2 * devices, *own.shape[1:]), stations)
    shape = jax.ShapeDtypeStruct((2, bins, 64, 128), jnp.bfloat16)
    total = None
    start = 0
    for part in woven:
        blocks = exchange(product(gather(part), scaling, devices))
        if total is not None:
            total, blocks = lax.optimization_barrier((total, blocks))
        given = swap(blocks)
        total = place_blocks(blocks, total, start, shape, True)
        total = place_blocks(given, total, start, shape, False)
        start += part.shape[1] * devices
    return total


def solution(mesh):
    placed = (P(AXES, None, None), P(AXES, None), P(), P())
    return jax.shard_map(
        body, mesh=mesh, in_specs=placed, out_specs=P(None, None, "row", "col"), check_vma=False
    )
```
